256 devices in a mesh: resp: 64 (over y_hi, x, z), head: 4 (over y_lo, core).
Axes of the slice: x: 4, y: 4 (y_hi: 2, y_lo: 2; y = y_hi * 2 + y_lo), z: 8, core: 2. Of those that a mesh axis runs over, the one named last changes fastest.
Arguments:
- queries: bfloat16 [16384, 8192], P('resp', 'head'), may hold values from -240 to 240
- d_out: bfloat16 [16384, 8192], P('resp', 'head'), may hold values from -24 to 24
- prefix_keys: bfloat16 [1024, 1024], P('resp', 'head'), may hold values from -17 to 17
- prefix_values: bfloat16 [1024, 1024], P('resp', 'head'), may hold values from -6 to 6
- k_weight: bfloat16 [8192, 1024], P(None, 'head'), may hold values from -0.0625 to 0.0625
- v_weight: bfloat16 [8192, 1024], P(None, 'head'), may hold values from -0.0625 to 0.0625
- lengths: int32 [64], P('resp'), may hold values from 1 to 256, as said below
Outputs:
- prefix_dk: bfloat16 [1024, 1024], P('resp', 'head')
- prefix_dv: bfloat16 [1024, 1024], P('resp', 'head')
- input_grad: bfloat16 [1024, 8192], P('resp', 'head')
The draws below stay inside these ranges and needn't reach their ends.
Inputs may be any that keep to these rules, and one draw needn't show every extreme that they name: `lengths`: every response has at least one live token and one response has exactly 256.
All inputs are finite; a program needn't handle non-finite values.
Results may differ from the reference program's by a relative error of at most 0.015.
Values may be sent and summed in bfloat16 or wider, within the bound.
A program may use at most 128 MiB of HBM per device.

```python
import jax
import jax.numpy as jnp
from jax import lax

D = 8192
HEADS = 64
KV = 8
HD = 128
LEN = 256
RESPONSES = 64
ROWS = 16384
PREFIX = 1024


def shared_keys(key, spread):
    base = jnp.clip(jax.random.normal(jax.random.fold_in(key, 101), (PREFIX, KV * HD), jnp.float32), -6.0, 6.0)
    logs = jax.random.uniform(jax.random.fold_in(key, 102), (PREFIX, 1), jnp.float32, -spread, spread)
    return base * jnp.exp(logs)


def draw_prefix_keys(key, part):
    spread = 0.0
    return shared_keys(key, spread).astype(jnp.bfloat16)


def draw_queries(key, part):
    key = jax.random.fold_in(key, 7)
    entries = jnp.clip(jax.random.normal(key, (ROWS, HEADS * HD), jnp.float32), -6.0, 6.0)
    return entries.astype(jnp.bfloat16)


def draw_lengths(key, part):
    key = jax.random.fold_in(key, 11)
    drawn = jax.random.randint(key, (RESPONSES,), 1, LEN + 1)
    chosen = jax.random.randint(jax.random.fold_in(key, 1), (), 0, RESPONSES)
    return drawn.at[chosen].set(LEN).astype(jnp.int32)


def shard_levels(own_key, shape, shards, least, high):
    loudness = 1.0
    for dim, parts in shards:
        steps = jax.random.uniform(jax.random.fold_in(jax.random.fold_in(own_key, 6), dim), (parts,), jnp.float32, least / len(shards), high / len(shards))
        loudness = loudness * jnp.repeat(jnp.exp(steps), shape[dim] // parts).reshape((-1,) + (1,) * (len(shape) - 1 - dim))
    return loudness


def scatter_about(stream_key, dims, deviation, reach, shards=(), kind=jnp.bfloat16):
    factor_of = shard_levels(stream_key, dims, shards, -0.22, 0.18) if shards else 1.0
    array = jax.random.normal(stream_key, dims, jnp.float32) * deviation * factor_of
    return jnp.minimum(jnp.maximum(array, -reach), reach).astype(kind)


def setup_inputs(seed: int = 0) -> dict:
    streams_of = jax.random.split(jax.random.key(seed), 8)
    return {
        "queries": draw_queries(jax.random.fold_in(streams_of[7], 71), 0),
        "d_out": scatter_about(streams_of[1], (ROWS, HEADS * HD), 4.0, 24.0, ((0, 64), (1, 4))),
        "prefix_keys": draw_prefix_keys(jax.random.fold_in(streams_of[7], 71), 0),
        "prefix_values": scatter_about(streams_of[3], (PREFIX, KV * HD), 1.0, 6.0, ((0, 64), (1, 4))),
        "k_weight": scatter_about(streams_of[4], (D, KV * HD), D ** -0.5, 0.0625, ((1, 4),)),
        "v_weight": scatter_about(streams_of[5], (D, KV * HD), D ** -0.5, 0.0625, ((1, 4),)),
        "lengths": draw_lengths(jax.random.fold_in(streams_of[7], 71), 0),
    }


def reference(queries, d_out, prefix_keys, prefix_values, k_weight, v_weight, lengths):
    group = HEADS // KV
    scale = HD ** -0.5
    keys = prefix_keys.astype(jnp.float32).reshape(PREFIX, KV, HD)
    values = prefix_values.astype(jnp.float32).reshape(PREFIX, KV, HD)
    query_blocks = queries.reshape(RESPONSES, LEN, KV, group, HD)
    grad_blocks = d_out.reshape(RESPONSES, LEN, KV, group, HD)

    def one_response(carry, inputs):
        query, grad, length = inputs
        live = jnp.arange(LEN, dtype=jnp.int32) < length
        grad = jnp.where(live[:, None, None, None], grad, jnp.zeros_like(grad))
        query_f = query.astype(jnp.float32)
        grad_f = grad.astype(jnp.float32)
        scores = jnp.einsum('tkgd,skd->tkgs', query_f, keys) * scale
        top = jnp.max(scores, axis=-1, keepdims=True)
        lse = top + jnp.log(jnp.sum(jnp.exp(scores - top), axis=-1, keepdims=True))
        probs = jnp.exp(scores - lse)
        dprobs = jnp.einsum('tkgd,skd->tkgs', grad_f, values)
        delta = jnp.sum(probs * dprobs, axis=-1, keepdims=True)
        probs_low = lax.optimization_barrier(probs.astype(jnp.bfloat16)).astype(jnp.float32)
        grad_v = jnp.einsum('tkgs,tkgd->skd', probs_low, grad_f)
        dscores = (probs * (dprobs - delta) * scale).astype(jnp.bfloat16)
        dscores = lax.optimization_barrier(dscores).astype(jnp.float32)
        grad_k = jnp.einsum('tkgs,tkgd->skd', dscores, query_f)
        return (carry[0] + grad_k, carry[1] + grad_v), None

    zeros = jnp.zeros((PREFIX, KV, HD), jnp.float32)
    (grad_k, grad_v), _ = lax.scan(one_response, (zeros, zeros), (query_blocks, grad_blocks, lengths))
    dk_low = grad_k.reshape(PREFIX, KV * HD).astype(jnp.bfloat16)
    dv_low = grad_v.reshape(PREFIX, KV * HD).astype(jnp.bfloat16)
    input_grad = jnp.dot(dk_low, k_weight.T, preferred_element_type=jnp.float32)
    input_grad = input_grad + jnp.dot(dv_low, v_weight.T, preferred_element_type=jnp.float32)
    return dk_low, dv_low, input_grad.astype(jnp.bfloat16)
```

```python
import functools
import math

import jax
import jax.numpy as jnp
from jax import lax
from jax.experimental import pallas as pl
from jax.experimental.pallas import tpu as pltpu
from jax.sharding import PartitionSpec as P

HD = 128
NY, NX, NZ = 2, 4, 8
NC = 2
N = 8
MESH = pl.DeviceIdType.MESH
SCALE = HD ** (-0.5)
LOG2E = math.log2(math.e)
F32 = jnp.float32
BF16 = jnp.bfloat16


def place():
    r = lax.axis_index("resp")
    return r // (NX * NZ), (r // NZ) % NX, r % NZ, lax.axis_index("head")


def xy_peer(i):
    y, x, z, h = place()
    return ((y + i // NX) % NY * (NX * NZ) + (x + i % NX) % NX * NZ + z, h)


def xy_back(i):
    return i // NX * NX + (-i) % NX


def z_peer(i):
    y, x, z, h = place()
    return (y * (NX * NZ) + x * NZ + (z + i) % NZ, h)


def z_back(i):
    return (-i) % NZ


XY = (xy_peer, xy_back)
Z = (z_peer, z_back)


def head_peer(i):
    y, x, z, h = place()
    return (lax.axis_index("resp"), (h // NC + i // NC) % 2 * NC + (h + i) % NC)


def nt(a, b):
    return lax.dot_general(a, b, (((1,), (1,)), ((), ())), preferred_element_type=F32)


def send(src, dst, ss, rs, to):
    copy = pltpu.make_async_remote_copy(
        src_ref=src, dst_ref=dst, send_sem=ss, recv_sem=rs, device_id=to, device_id_type=MESH
    )
    copy.start()
    return copy


def kernel(
    q_hbm, g_hbm, k_hbm, v_hbm, kw_hbm, vw_hbm, len_ref,
    dk_ref, dv_ref, in_ref,
    qs, gs, kw, vw, full, outbox, inbox, partial, inbox2, low,
    e_s, dp_s, m_s, l_s, w_s, p_s, ds_s, hsend, hrecv, hown,
    load_sem, own_sem, w_sem, ss, rs, hss, hrs,
):
    heads = qs.shape[0]
    group = heads // 2
    rows = qs.shape[1]

    barrier = pltpu.get_barrier_semaphore()
    for peer, _ in (XY, Z):
        for i in range(1, N):
            pl.semaphore_signal(barrier, inc=1, device_id=peer(i), device_id_type=MESH)
    for i in range(1, 4):
        pl.semaphore_signal(barrier, inc=1, device_id=head_peer(i), device_id_type=MESH)

    own = []
    for j in range(2):
        cols = pl.ds(j * HD, HD)
        own.append(pltpu.make_async_copy(k_hbm.at[:, cols], full.at[j, 0, 0, :, pl.ds(0, HD)], own_sem.at[2 * j]))
        own.append(pltpu.make_async_copy(v_hbm.at[:, cols], full.at[j, 0, 0, :, pl.ds(HD, HD)], own_sem.at[2 * j + 1]))
    for copy in own:
        copy.start()
    loads = []
    for h in range(heads):
        cols = pl.ds(h * HD, HD)
        loads.append(pltpu.make_async_copy(q_hbm.at[:, cols], qs.at[h], load_sem.at[0, h]))
        loads.append(pltpu.make_async_copy(g_hbm.at[:, cols], gs.at[h], load_sem.at[1, h]))
    for copy in loads:
        copy.start()
    weights = [
        pltpu.make_async_copy(kw_hbm, kw, w_sem.at[0]),
        pltpu.make_async_copy(vw_hbm, vw, w_sem.at[1]),
    ]
    for copy in weights:
        copy.start()
    for copy in own:
        copy.wait()
    pl.semaphore_wait(barrier, 2 * (N - 1) + 3)

    first = (XY, Z)
    second = (Z, XY)
    sent = []

    def fan(step, j, axes, src_of, dst_of):
        peer, back = axes
        copies = []
        for i in range(1, N):
            copies.append(
                send(src_of(i), dst_of(back(i)), ss.at[step, j, i], rs.at[step, j, back(i)], peer(i))
            )
        sent.extend(copies)
        return copies

    gather1 = [
        fan(0, j, first[j], lambda i, j=j: full.at[j, 0, 0], lambda b, j=j: full.at[j, 0, b]) for j in range(2)
    ]
    gather2 = []
    for j in range(2):
        for copy in gather1[j]:
            copy.wait_recv()
        gather2.append(
            fan(1, j, second[j], lambda i, j=j: full.at[j, 0], lambda b, j=j: full.at[j, b])
        )

    for copy in loads:
        copy.wait()
    live = lax.broadcasted_iota(jnp.int32, (rows, HD), 0) < len_ref[0]

    def mask(h, carry):
        grad = gs[h]
        gs[h] = jnp.where(live, grad.astype(F32), 0.0).astype(BF16)
        return carry

    lax.fori_loop(0, heads, mask, 0)

    def attend(j):
        def one(h, carry):
            q = qs[j * group + h]
            g = gs[j * group + h]
            for c in range(N):
                kv = full[j, c].reshape(N * 16, 2 * HD)
                s = nt(kv[:, :HD], q) * (SCALE * LOG2E)
                dp = nt(kv[:, HD:], g)
                m = jnp.max(s, axis=0, keepdims=True)
                e = jnp.exp2(s - m)
                m_s[c] = m
                l_s[c] = jnp.sum(e, axis=0, keepdims=True)
                w_s[c] = jnp.sum(e * dp, axis=0, keepdims=True)
                e_s[c] = e
                dp_s[c] = dp
            m = m_s[...]
            f = jnp.exp2(m - jnp.max(m, axis=0, keepdims=True))
            total = jnp.sum(f * l_s[...], axis=0)
            delta = jnp.sum(f * w_s[...], axis=0) / total
            m_s[...] = f / total[None]
            for c in range(N):
                p = e_s[c] * m_s[c]
                p_s[h, c] = p.astype(BF16)
                ds_s[h, c] = (p * (dp_s[c] - delta)).astype(BF16)
            return carry

        lax.fori_loop(0, group, one, 0)

        def products(c, carry):
            dv = jnp.zeros((N * 16, HD), F32)
            dk = jnp.zeros((N * 16, HD), F32)
            for h in range(group):
                dv += jnp.dot(p_s[h, c], gs[j * group + h], preferred_element_type=F32)
                dk += jnp.dot(ds_s[h, c], qs[j * group + h], preferred_element_type=F32)
            outbox[j, c, :, :, :HD] = (dk * SCALE).astype(BF16).reshape(N, 16, HD)
            outbox[j, c, :, :, HD:] = dv.astype(BF16).reshape(N, 16, HD)
            return carry

        lax.fori_loop(0, N, products, 0)
        return fan(2, j, second[j], lambda i: outbox.at[j, i], lambda b: inbox.at[j, b])

    def reduce1(j, copies):
        for copy in copies:
            copy.wait_recv()
        total = outbox[j, 0].astype(F32)
        for i in range(1, N):
            total += inbox[j, i].astype(F32)
        partial[j] = total.astype(BF16)
        return fan(3, j, first[j], lambda i: partial.at[j, i], lambda b: inbox2.at[j, b])

    def reduce2(j, copies):
        for copy in copies:
            copy.wait_recv()
        total = partial[j, 0].astype(F32)
        for i in range(1, N):
            total += inbox2[j, i].astype(F32)
        total = total.astype(BF16)
        cols = slice(j * HD, (j + 1) * HD)
        low[0, :, cols] = total[:, :HD]
        low[1, :, cols] = total[:, HD:]
        dk_ref[:, cols] = total[:, :HD]
        dv_ref[:, cols] = total[:, HD:]

    for copy in gather2[1]:
        copy.wait_recv()
    scatter_b = attend(1)
    for copy in gather2[0]:
        copy.wait_recv()
    scatter_b = reduce1(1, scatter_b)
    scatter_a = attend(0)
    reduce2(1, scatter_b)
    scatter_a = reduce1(0, scatter_a)
    for copy in weights:
        copy.wait()
    reduce2(0, scatter_a)

    width = hown.shape[1]
    step = 512
    me = lax.axis_index("head")
    low_k = low[0]
    low_v = low[1]
    exchange = []
    for i in (2, 3, 1, 0):
        _, dest = head_peer(i)
        for t in range(width // step):
            span = pl.ds(pl.multiple_of(dest * width + t * step, step), step)
            part = nt(low_k, kw[span, :]) + nt(low_v, vw[span, :])
            if i:
                hsend[i - 1, :, t * step:(t + 1) * step] = part.astype(BF16)
            else:
                hown[:, t * step:(t + 1) * step] = part
        if i:
            exchange.append(
                send(hsend.at[i - 1], hrecv.at[i - 1], hss.at[i - 1], hrs.at[i - 1], head_peer(i))
            )
    total = hown[...]
    for copy in exchange:
        copy.wait_recv()
    for i in range(3):
        total += hrecv[i].astype(F32)
    in_ref[...] = total.astype(BF16)
    for copy in sent + exchange:
        copy.wait_send()


def body(queries, d_out, prefix_keys, prefix_values, k_weight, v_weight, lengths):
    rows, width = queries.shape
    heads = width // HD
    d = k_weight.shape[0]
    any_spec = pl.BlockSpec(memory_space=pl.ANY)
    vmem = pl.BlockSpec(memory_space=pltpu.VMEM)
    shard = jax.ShapeDtypeStruct(prefix_keys.shape, BF16)
    return pl.pallas_call(
        kernel,
        name="prefix_gradients",
        out_shape=(shard, shard, jax.ShapeDtypeStruct((16, d // 4), BF16)),
        in_specs=[any_spec] * 6 + [pl.BlockSpec(memory_space=pltpu.SMEM)],
        out_specs=(vmem, vmem, vmem),
        scratch_shapes=[
            pltpu.VMEM((heads, rows, HD), BF16),
            pltpu.VMEM((heads, rows, HD), BF16),
            pltpu.VMEM(k_weight.shape, BF16),
            pltpu.VMEM(v_weight.shape, BF16),
            pltpu.VMEM((2, N, N, 16, 2 * HD), BF16),
            pltpu.VMEM((2, N, N, 16, 2 * HD), BF16),
            pltpu.VMEM((2, N, N, 16, 2 * HD), BF16),
            pltpu.VMEM((2, N, 16, 2 * HD), BF16),
            pltpu.VMEM((2, N, 16, 2 * HD), BF16),
            pltpu.VMEM((2, 16, 2 * HD), BF16),
            pltpu.VMEM((N, N * 16, rows), F32),
            pltpu.VMEM((N, N * 16, rows), F32),
            pltpu.VMEM((N, 1, rows), F32),
            pltpu.VMEM((N, 1, rows), F32),
            pltpu.VMEM((N, 1, rows), F32),
            pltpu.VMEM((heads // 2, N, N * 16, rows), BF16),
            pltpu.VMEM((heads // 2, N, N * 16, rows), BF16),
            pltpu.VMEM((3, 16, d // 4), BF16),
            pltpu.VMEM((3, 16, d // 4), BF16),
            pltpu.VMEM((16, d // 4), F32),
            pltpu.SemaphoreType.DMA((2, heads)),
            pltpu.SemaphoreType.DMA((4,)),
            pltpu.SemaphoreType.DMA((2,)),
            pltpu.SemaphoreType.DMA((4, 2, N)),
            pltpu.SemaphoreType.DMA((4, 2, N)),
            pltpu.SemaphoreType.DMA((3,)),
            pltpu.SemaphoreType.DMA((3,)),
        ],
        compiler_params=pltpu.CompilerParams(
            collective_id=0, has_side_effects=True, vmem_limit_bytes=48 * 1024 * 1024
        ),
    )(queries, d_out, prefix_keys, prefix_values, k_weight, v_weight, lengths)


def solution(mesh):
    placed = (
        P("resp", "head"),
        P("resp", "head"),
        P("resp", "head"),
        P("resp", "head"),
        P(None, "head"),
        P(None, "head"),
        P("resp"),
    )
    return jax.shard_map(
        body,
        mesh=mesh,
        in_specs=placed,
        out_specs=(P("resp", "head"), P("resp", "head"), P("resp", "head")),
        check_vma=False,
    )
```

```python
import functools
import math

import jax
import jax.numpy as jnp
from jax import lax
from jax.experimental import pallas as pl
from jax.experimental.pallas import tpu as pltpu
from jax.sharding import PartitionSpec as P

HD = 128
NY, NX, NZ = 2, 4, 8
NC = 2
N = 8
MESH = pl.DeviceIdType.MESH
SCALE = HD ** (-0.5)
LOG2E = math.log2(math.e)
F32 = jnp.float32
BF16 = jnp.bfloat16


def place():
    r = lax.axis_index("resp")
    return r // (NX * NZ), (r // NZ) % NX, r % NZ, lax.axis_index("head")


def xy_peer(i):
    y, x, z, h = place()
    return ((y + i // NX) % NY * (NX * NZ) + (x + i % NX) % NX * NZ + z, h)


def xy_back(i):
    return i // NX * NX + (-i) % NX


def z_peer(i):
    y, x, z, h = place()
    return (y * (NX * NZ) + x * NZ + (z + i) % NZ, h)


def z_back(i):
    return (-i) % NZ


XY = (xy_peer, xy_back)
Z = (z_peer, z_back)


def head_peer(i):
    y, x, z, h = place()
    return (lax.axis_index("resp"), (h // NC + i // NC) % 2 * NC + (h + i) % NC)


def nt(a, b):
    return lax.dot_general(a, b, (((1,), (1,)), ((), ())), preferred_element_type=F32)


def send(src, dst, ss, rs, to):
    copy = pltpu.make_async_remote_copy(
        src_ref=src, dst_ref=dst, send_sem=ss, recv_sem=rs, device_id=to, device_id_type=MESH
    )
    copy.start()
    return copy


def kernel(
    q_hbm, g_hbm, k_hbm, v_hbm, kw_hbm, vw_hbm, len_ref,
    dk_ref, dv_ref, mine_ref, theirs_ref,
    qs, gs, wts, full, outbox, inbox, partial, inbox2, low, acc,
    e_s, dp_s, m_s, l_s, w_s, d_s, hsend,
    load_sem, own_sem, w_sem, ss, rs, hss, hrs,
):
    heads = qs.shape[0]
    group = heads // 2
    rows = qs.shape[1]

    barrier = pltpu.get_barrier_semaphore()
    for peer, _ in (XY, Z):
        for i in range(1, N):
            pl.semaphore_signal(barrier, inc=1, device_id=peer(i), device_id_type=MESH)
    for i in range(1, 4):
        pl.semaphore_signal(barrier, inc=1, device_id=head_peer(i), device_id_type=MESH)

    own = []
    for j in range(2):
        cols = pl.ds(j * HD, HD)
        own.append(pltpu.make_async_copy(k_hbm.at[:, cols], full.at[j, 0, 0, :, pl.ds(0, HD)], own_sem.at[2 * j]))
        own.append(pltpu.make_async_copy(v_hbm.at[:, cols], full.at[j, 0, 0, :, pl.ds(HD, HD)], own_sem.at[2 * j + 1]))
    for copy in own:
        copy.start()
    loads = []
    for h in range(heads):
        cols = pl.ds(h * HD, HD)
        loads.append(pltpu.make_async_copy(q_hbm.at[:, cols], qs.at[h], load_sem.at[0, h]))
        loads.append(pltpu.make_async_copy(g_hbm.at[:, cols], gs.at[h], load_sem.at[1, h]))
    for copy in loads:
        copy.start()
    weights = []
    for j in (1, 0):
        for i, ref in enumerate((kw_hbm, vw_hbm)):
            weights.append(
                pltpu.make_async_copy(ref.at[:, pl.ds(j * HD, HD)], wts.at[j, :, pl.ds(i * HD, HD)], w_sem.at[j, i])
            )
    for copy in weights:
        copy.start()
    for copy in own:
        copy.wait()
    pl.semaphore_wait(barrier, 2 * (N - 1) + 3)

    sent = []

    def fan(step, j, axes, src_of, dst_of):
        peer, back = axes
        copies = []
        for i in range(1, N):
            copies.append(
                send(src_of(i), dst_of(back(i)), ss.at[step, j, i], rs.at[step, j, back(i)], peer(i))
            )
        sent.extend(copies)
        return copies

    spread_b = fan(0, 1, Z, lambda i: full.at[1, 0, 0], lambda b: full.at[1, 0, b])
    spread_a = fan(0, 0, XY, lambda i: full.at[0, 0, 0], lambda b: full.at[0, b, 0])
    for copy in spread_b:
        copy.wait_recv()
    fan(1, 1, XY, lambda i: full.at[1, 0], lambda b: full.at[1, b])
    for copy in spread_a:
        copy.wait_recv()
    blocks_a = fan(1, 0, Z, lambda i: full.at[0, :, 0], lambda b: full.at[0, :, b])

    for copy in loads:
        copy.wait()
    live = lax.broadcasted_iota(jnp.int32, (rows, HD), 0) < len_ref[0]

    def mask(h, carry):
        grad = gs[h]
        gs[h] = jnp.where(live, grad.astype(F32), 0.0).astype(BF16)
        return carry

    lax.fori_loop(0, heads, mask, 0)

    def softmax_terms(j, c):
        kv = full[j, c].reshape(N * 16, 2 * HD)
        for h in range(group):
            s = nt(kv[:, :HD], qs[j * group + h]) * (SCALE * LOG2E)
            dp = nt(kv[:, HD:], gs[j * group + h])
            m = jnp.max(s, axis=0, keepdims=True)
            e = jnp.exp2(s - m)
            m_s[h, pl.ds(c, 1)] = m
            l_s[h, pl.ds(c, 1)] = jnp.sum(e, axis=0, keepdims=True)
            w_s[h, pl.ds(c, 1)] = jnp.sum(e * dp, axis=0, keepdims=True)
            e_s[h, c] = e
            dp_s[h, c] = dp

    def combine():
        m = m_s[...]
        f = jnp.exp2(m - jnp.max(m, axis=1, keepdims=True))
        total = jnp.sum(f * l_s[...], axis=1, keepdims=True)
        d_s[...] = jnp.sum(f * w_s[...], axis=1, keepdims=True) / total
        m_s[...] = f / total

    def block(j, c):
        back = c // NX * NX + (NX - c % NX) % NX
        return pltpu.make_async_remote_copy(
            src_ref=outbox.at[j, c], dst_ref=inbox.at[j, back],
            send_sem=ss.at[2, j, c], recv_sem=rs.at[2, j, back],
            device_id=xy_peer(c), device_id_type=MESH,
        )

    def gradients(j):
        queries = qs[j * group:(j + 1) * group].reshape(group * rows, HD)
        grads = gs[j * group:(j + 1) * group].reshape(group * rows, HD)

        def one(step, carry):
            c = N - 1 - step
            probs = []
            dscores = []
            for h in range(group):
                p = e_s[h, c] * m_s[h, pl.ds(c, 1)]
                probs.append(p.astype(BF16))
                dscores.append((p * (dp_s[h, c] - d_s[h])).astype(BF16))
            dv = jnp.dot(jnp.concatenate(probs, axis=1), grads, preferred_element_type=F32)
            dk = jnp.dot(jnp.concatenate(dscores, axis=1), queries, preferred_element_type=F32)
            outbox[j, c, :, :, :HD] = (dk * SCALE).astype(BF16).reshape(N, 16, HD)
            outbox[j, c, :, :, HD:] = dv.astype(BF16).reshape(N, 16, HD)

            @pl.when(c > 0)
            def _():
                block(j, c).start()

            return carry

        lax.fori_loop(0, N, one, 0)

    def reduce1(j):
        total = outbox[j, 0].astype(F32)
        for i in range(N - 1, 0, -1):
            block(j, i).wait_recv()
            total += inbox[j, xy_back(i)].astype(F32)
        partial[j] = total.astype(BF16)
        return fan(3, j, Z, lambda i: partial.at[j, i], lambda b: inbox2.at[j, b])

    def reduce2(j, copies):
        total = partial[j, 0].astype(F32)
        for i, copy in enumerate(copies):
            copy.wait_recv()
            total += inbox2[j, z_back(i + 1)].astype(F32)
        total = total.astype(BF16)
        cols = slice(j * HD, (j + 1) * HD)
        low[j] = total
        dk_ref[:, cols] = total[:, :HD]
        dv_ref[:, cols] = total[:, HD:]

    def stream(c, carry):
        @pl.when(c > 0)
        def _():
            pltpu.make_async_remote_copy(
                src_ref=full.at[1, 0], dst_ref=full.at[1, c],
                send_sem=ss.at[1, 1, c], recv_sem=rs.at[1, 1, c],
                device_id=xy_peer(c), device_id_type=MESH,
            ).wait_recv()

        softmax_terms(1, c)
        return carry

    lax.fori_loop(0, N, stream, 0)
    combine()
    gradients(1)
    for copy in blocks_a:
        copy.wait_recv()

    def whole(c, carry):
        softmax_terms(0, c)
        return carry

    lax.fori_loop(0, N, whole, 0)
    combine()
    sums_b = reduce1(1)
    gradients(0)
    sums_a = reduce1(0)
    reduce2(1, sums_b)
    for copy in weights:
        copy.wait()

    width = acc.shape[1] // 4
    step = 512
    low_b = low[1]

    def project(t, carry):
        span = pl.ds(pl.multiple_of(t * step, step), step)
        acc[:, span] = nt(low_b, wts[1, span, :])
        return carry

    lax.fori_loop(0, 4 * width // step, project, 0)
    reduce2(0, sums_a)
    low_a = low[0]
    exchange = []
    for i in (2, 3, 1, 0):
        _, dest = head_peer(i)
        for t in range(width // step):
            span = pl.ds(pl.multiple_of(dest * width + t * step, step), step)
            part = acc[:, span] + nt(low_a, wts[0, span, :])
            if i:
                hsend[i - 1, :, t * step:(t + 1) * step] = part.astype(BF16)
            else:
                mine_ref[:, t * step:(t + 1) * step] = part
        if i:
            exchange.append(
                send(hsend.at[i - 1], theirs_ref.at[i - 1], hss.at[i - 1], hrs.at[i - 1], head_peer(i))
            )
    for copy in exchange:
        copy.wait_recv()
    for copy in sent + exchange:
        copy.wait_send()

    def flushed(c, carry):
        block(0, c).wait_send()
        block(1, c).wait_send()
        return carry

    lax.fori_loop(1, N, flushed, 0)


def finish(dk_ref, dv_ref, mine_ref, theirs_ref, dk_out, dv_out, in_out):
    dk_out[...] = dk_ref[...]
    dv_out[...] = dv_ref[...]
    total = mine_ref[...]
    for i in range(3):
        total += theirs_ref[i].astype(F32)
    in_out[...] = total.astype(BF16)


def body(queries, d_out, prefix_keys, prefix_values, k_weight, v_weight, lengths):
    rows, width = queries.shape
    heads = width // HD
    d = k_weight.shape[0]
    hbm = pl.BlockSpec(memory_space=pltpu.HBM)
    vmem = pl.BlockSpec(memory_space=pltpu.VMEM)
    shard = jax.ShapeDtypeStruct(prefix_keys.shape, BF16)
    parts = pl.pallas_call(
        kernel,
        name="prefix_gradients",
        out_shape=(
            shard,
            shard,
            jax.ShapeDtypeStruct((16, d // 4), F32),
            jax.ShapeDtypeStruct((3, 16, d // 4), BF16),
        ),
        in_specs=[hbm] * 6 + [pl.BlockSpec(memory_space=pltpu.SMEM)],
        out_specs=(vmem,) * 4,
        scratch_shapes=[
            pltpu.VMEM((heads, rows, HD), BF16),
            pltpu.VMEM((heads, rows, HD), BF16),
            pltpu.VMEM((2, d, 2 * HD), BF16),
            pltpu.VMEM((2, N, N, 16, 2 * HD), BF16),
            pltpu.VMEM((2, N, N, 16, 2 * HD), BF16),
            pltpu.VMEM((2, N, N, 16, 2 * HD), BF16),
            pltpu.VMEM((2, N, 16, 2 * HD), BF16),
            pltpu.VMEM((2, N, 16, 2 * HD), BF16),
            pltpu.VMEM((2, 16, 2 * HD), BF16),
            pltpu.VMEM((16, d), F32),
            pltpu.VMEM((heads // 2, N, N * 16, rows), F32),
            pltpu.VMEM((heads // 2, N, N * 16, rows), F32),
            pltpu.VMEM((heads // 2, N, rows), F32),
            pltpu.VMEM((heads // 2, N, rows), F32),
            pltpu.VMEM((heads // 2, N, rows), F32),
            pltpu.VMEM((heads // 2, 1, rows), F32),
            pltpu.VMEM((3, 16, d // 4), BF16),
            pltpu.SemaphoreType.DMA((2, heads)),
            pltpu.SemaphoreType.DMA((4,)),
            pltpu.SemaphoreType.DMA((2, 2)),
            pltpu.SemaphoreType.DMA((4, 2, N)),
            pltpu.SemaphoreType.DMA((4, 2, N)),
            pltpu.SemaphoreType.DMA((3,)),
            pltpu.SemaphoreType.DMA((3,)),
        ],
        compiler_params=pltpu.CompilerParams(
            collective_id=0, has_side_effects=True, vmem_limit_bytes=60 * 1024 * 1024
        ),
    )(queries, d_out, prefix_keys, prefix_values, k_weight, v_weight, lengths)
    return pl.pallas_call(
        finish,
        name="sum_of_heads",
        out_shape=(shard, shard, jax.ShapeDtypeStruct((16, d // 4), BF16)),
        in_specs=[vmem] * 4,
        out_specs=(vmem,) * 3,
    )(*parts)


def solution(mesh):
    placed = (
        P("resp", "head"),
        P("resp", "head"),
        P("resp", "head"),
        P("resp", "head"),
        P(None, "head"),
        P(None, "head"),
        P("resp"),
    )
    return jax.shard_map(
        body,
        mesh=mesh,
        in_specs=placed,
        out_specs=(P("resp", "head"), P("resp", "head"), P("resp", "head")),
        check_vma=False,
    )
```

```python
import functools
import math

import jax
import jax.numpy as jnp
from jax import lax
from jax.experimental import pallas as pl
from jax.experimental.pallas import tpu as pltpu
from jax.sharding import PartitionSpec as P

HD = 128
NY, NX, NZ = 2, 4, 8
NC = 2
CHUNK = 128
N = 8
MESH = pl.DeviceIdType.MESH
SCALE = HD ** (-0.5)
LOG2E = math.log2(math.e)
F32 = jnp.float32
BF16 = jnp.bfloat16


def place():
    r = lax.axis_index("resp")
    return r // (NX * NZ), (r // NZ) % NX, r % NZ, lax.axis_index("head")


def xy_peer(i):
    y, x, z, h = place()
    return ((y + i // NX) % NY * (NX * NZ) + (x + i % NX) % NX * NZ + z, h)


def xy_back(i):
    return i // NX * NX + (-i) % NX


def z_peer(i):
    y, x, z, h = place()
    return (y * (NX * NZ) + x * NZ + (z + i) % NZ, h)


def z_back(i):
    return (-i) % NZ


XY = (xy_peer, xy_back)
Z = (z_peer, z_back)


def head_peer(i):
    y, x, z, h = place()
    return (lax.axis_index("resp"), (h // NC + i // NC) % 2 * NC + (h + i) % NC)


def nt(a, b):
    return lax.dot_general(a, b, (((1,), (1,)), ((), ())), preferred_element_type=F32)


def send(src, dst, ss, rs, to):
    copy = pltpu.make_async_remote_copy(
        src_ref=src, dst_ref=dst, send_sem=ss, recv_sem=rs, device_id=to, device_id_type=MESH
    )
    copy.start()
    return copy


def kernel(
    q_hbm, g_hbm, k_hbm, v_hbm, kw_hbm, vw_hbm, len_hbm,
    dk_ref, dv_ref, mine_ref, theirs_ref,
    qs, gs, wts, full, outbox, inbox, partial, inbox2, low, acc,
    e_s, dp_s, m_s, l_s, w_s, d_s, hsend, len_ref,
    load_sem, own_sem, w_sem, ss, rs, hss, hrs,
):
    rows, columns = qs.shape
    group = columns // HD // 2

    barrier = pltpu.get_barrier_semaphore()
    for peer, _ in (XY, Z):
        for i in range(1, N):
            pl.semaphore_signal(barrier, inc=1, device_id=peer(i), device_id_type=MESH)
    for i in range(1, 4):
        pl.semaphore_signal(barrier, inc=1, device_id=head_peer(i), device_id_type=MESH)

    own = []
    for j in range(2):
        cols = pl.ds(j * HD, HD)
        own.append(pltpu.make_async_copy(k_hbm.at[:, cols], full.at[j, 0, 0, :, pl.ds(0, HD)], own_sem.at[2 * j]))
        own.append(pltpu.make_async_copy(v_hbm.at[:, cols], full.at[j, 0, 0, :, pl.ds(HD, HD)], own_sem.at[2 * j + 1]))
    for copy in own:
        copy.start()
    loads = [
        pltpu.make_async_copy(q_hbm, qs, load_sem.at[0]),
        pltpu.make_async_copy(g_hbm, gs, load_sem.at[1]),
        pltpu.make_async_copy(len_hbm, len_ref, load_sem.at[2]),
    ]
    for copy in loads:
        copy.start()
    weights = []
    for j in (1, 0):
        for i, ref in enumerate((kw_hbm, vw_hbm)):
            weights.append(
                pltpu.make_async_copy(ref.at[:, pl.ds(j * HD, HD)], wts.at[j, :, pl.ds(i * HD, HD)], w_sem.at[j, i])
            )
    for copy in weights:
        copy.start()
    for copy in own:
        copy.wait()
    pl.semaphore_wait(barrier, 2 * (N - 1) + 3)

    sent = []

    def fan(step, j, axes, src_of, dst_of):
        peer, back = axes
        copies = []
        for i in range(1, N):
            copies.append(
                send(src_of(i), dst_of(back(i)), ss.at[step, j, i], rs.at[step, j, back(i)], peer(i))
            )
        sent.extend(copies)
        return copies

    spread_b = fan(0, 1, Z, lambda i: full.at[1, 0, 0], lambda b: full.at[1, 0, b])
    spread_a = fan(0, 0, XY, lambda i: full.at[0, 0, 0], lambda b: full.at[0, b, 0])
    for copy in spread_b:
        copy.wait_recv()
    fan(1, 1, XY, lambda i: full.at[1, 0], lambda b: full.at[1, b])
    for copy in spread_a:
        copy.wait_recv()
    blocks_a = fan(1, 0, Z, lambda i: full.at[0, :, 0], lambda b: full.at[0, :, b])

    for copy in loads:
        copy.wait()
    length = len_ref[0]
    slab = 16

    def mask(i, carry):
        base = pl.multiple_of(i * slab, slab)
        live = lax.broadcasted_iota(jnp.int32, (slab, columns), 0) + base < length
        grad = gs[pl.ds(base, slab), :]
        gs[pl.ds(base, slab), :] = jnp.where(live, grad.astype(F32), 0.0).astype(BF16)
        return carry

    lax.fori_loop(0, rows // slab, mask, 0)

    def head(ref, j, h):
        return ref[:, (j * group + h) * HD:(j * group + h + 1) * HD]

    def stacked(ref, j):
        return jnp.concatenate([head(ref, j, h) for h in range(group)], axis=0)

    def softmax_terms(j, first, count):
        kv = full[j, pl.ds(first, count)].reshape(count * CHUNK, 2 * HD)
        for h in range(group):
            scores = nt(kv[:, :HD], head(qs, j, h)) * (SCALE * LOG2E)
            dprobs = nt(kv[:, HD:], head(gs, j, h))
            for i in range(count):
                c = first + i
                s = scores[i * CHUNK:(i + 1) * CHUNK]
                dp = dprobs[i * CHUNK:(i + 1) * CHUNK]
                m = jnp.max(s, axis=0, keepdims=True)
                e = jnp.exp2(s - m)
                m_s[h, pl.ds(c, 1)] = m
                l_s[h, pl.ds(c, 1)] = jnp.sum(e, axis=0, keepdims=True)
                w_s[h, pl.ds(c, 1)] = jnp.sum(e * dp, axis=0, keepdims=True)
                e_s[h, c] = e
                dp_s[h, c] = dp

    def combine():
        m = m_s[...]
        f = jnp.exp2(m - jnp.max(m, axis=1, keepdims=True))
        total = jnp.sum(f * l_s[...], axis=1, keepdims=True)
        d_s[...] = jnp.sum(f * w_s[...], axis=1, keepdims=True) / total
        m_s[...] = f / total

    def block(j, c):
        back = c // NX * NX + (NX - c % NX) % NX
        return pltpu.make_async_remote_copy(
            src_ref=outbox.at[j, c], dst_ref=inbox.at[j, back],
            send_sem=ss.at[2, j, c], recv_sem=rs.at[2, j, back],
            device_id=xy_peer(c), device_id_type=MESH,
        )

    def gradients(j, count):
        def one(step, carry):
            first = N - count * (step + 1)
            probs = []
            dscores = []
            for h in range(group):
                for i in range(count):
                    p = e_s[h, first + i] * m_s[h, pl.ds(first + i, 1)]
                    probs.append(p.astype(BF16))
                    dscores.append((p * (dp_s[h, first + i] - d_s[h])).astype(BF16))

            def whole(parts):
                columns = [jnp.concatenate(parts[h * count:(h + 1) * count], axis=0) for h in range(group)]
                return jnp.concatenate(columns, axis=1)

            dv = jnp.dot(whole(probs), stacked(gs, j), preferred_element_type=F32)
            dk = jnp.dot(whole(dscores), stacked(qs, j), preferred_element_type=F32)
            span = pl.ds(first, count)
            outbox[j, span, :, :, :HD] = (dk * SCALE).astype(BF16).reshape(count, N, 16, HD)
            outbox[j, span, :, :, HD:] = dv.astype(BF16).reshape(count, N, 16, HD)
            for i in range(count - 1, 0, -1):
                block(j, first + i).start()

            @pl.when(first > 0)
            def _():
                block(j, first).start()

            return carry

        lax.fori_loop(0, N // count, one, 0)

    def reduce1(j):
        total = outbox[j, 0].astype(F32)
        for i in range(N - 1, 0, -1):
            block(j, i).wait_recv()
            total += inbox[j, xy_back(i)].astype(F32)
        partial[j] = total.astype(BF16)
        return fan(3, j, Z, lambda i: partial.at[j, i], lambda b: inbox2.at[j, b])

    def reduce2(j, copies):
        total = partial[j, 0].astype(F32)
        for i, copy in enumerate(copies):
            copy.wait_recv()
            total += inbox2[j, z_back(i + 1)].astype(F32)
        total = total.astype(BF16)
        cols = slice(j * HD, (j + 1) * HD)
        low[j] = total
        dk_ref[:, cols] = total[:, :HD]
        dv_ref[:, cols] = total[:, HD:]

    def stream(c, carry):
        @pl.when(c > 0)
        def _():
            pltpu.make_async_remote_copy(
                src_ref=full.at[1, 0], dst_ref=full.at[1, c],
                send_sem=ss.at[1, 1, c], recv_sem=rs.at[1, 1, c],
                device_id=xy_peer(c), device_id_type=MESH,
            ).wait_recv()

        softmax_terms(1, c, 1)
        return carry

    lax.fori_loop(0, N, stream, 0)
    combine()
    gradients(1, 4)
    for copy in blocks_a:
        copy.wait_recv()

    def rest(i, carry):
        softmax_terms(0, i * 4, 4)
        return carry

    lax.fori_loop(0, N // 4, rest, 0)
    combine()
    gradients(0, 4)
    sums_b = reduce1(1)
    sums_a = reduce1(0)
    reduce2(1, sums_b)
    for copy in weights:
        copy.wait()

    def flush():
        for copy in sent[:-2 * (N - 1)]:
            copy.wait_send()

        def flushed(c, carry):
            block(1, c).wait_send()
            block(0, c).wait_send()
            return carry

        lax.fori_loop(1, N, flushed, 0)

    width = acc.shape[1] // 4
    step = 512
    low_b = low[1]

    def project(t, carry):
        span = pl.ds(pl.multiple_of(t * step, step), step)
        acc[:, span] = nt(low_b, wts[1, span, :])
        return carry

    lax.fori_loop(0, 4 * width // step, project, 0)
    flush()
    reduce2(0, sums_a)
    low_a = low[0]
    exchange = []
    for i in (2, 3, 1, 0):
        _, dest = head_peer(i)
        for t in range(width // step):
            span = pl.ds(pl.multiple_of(dest * width + t * step, step), step)
            part = acc[:, span] + nt(low_a, wts[0, span, :])
            if i:
                hsend[i - 1, :, t * step:(t + 1) * step] = part.astype(BF16)
            else:
                mine_ref[:, t * step:(t + 1) * step] = part
        if i:
            exchange.append(
                send(hsend.at[i - 1], theirs_ref.at[i - 1], hss.at[i - 1], hrs.at[i - 1], head_peer(i))
            )
    for copy in exchange:
        copy.wait_recv()
    for copy in sent[-2 * (N - 1):] + exchange:
        copy.wait_send()


def finish(dk_ref, dv_ref, mine_ref, theirs_ref, dk_out, dv_out, in_out):
    dk_out[...] = dk_ref[...]
    dv_out[...] = dv_ref[...]
    total = mine_ref[...]
    for i in range(3):
        total += theirs_ref[i].astype(F32)
    in_out[...] = total.astype(BF16)


def body(queries, d_out, prefix_keys, prefix_values, k_weight, v_weight, lengths):
    rows, width = queries.shape
    heads = width // HD
    d = k_weight.shape[0]
    hbm = pl.BlockSpec(memory_space=pltpu.HBM)
    vmem = pl.BlockSpec(memory_space=pltpu.VMEM)
    shard = jax.ShapeDtypeStruct(prefix_keys.shape, BF16)
    parts = pl.pallas_call(
        kernel,
        name="prefix_gradients",
        out_shape=(
            shard,
            shard,
            jax.ShapeDtypeStruct((16, d // 4), F32),
            jax.ShapeDtypeStruct((3, 16, d // 4), BF16),
        ),
        in_specs=[hbm] * 7,
        out_specs=(vmem,) * 4,
        scratch_shapes=[
            pltpu.VMEM((rows, width), BF16),
            pltpu.VMEM((rows, width), BF16),
            pltpu.VMEM((2, d, 2 * HD), BF16),
            pltpu.VMEM((2, N, N, 16, 2 * HD), BF16),
            pltpu.VMEM((2, N, N, 16, 2 * HD), BF16),
            pltpu.VMEM((2, N, N, 16, 2 * HD), BF16),
            pltpu.VMEM((2, N, 16, 2 * HD), BF16),
            pltpu.VMEM((2, N, 16, 2 * HD), BF16),
            pltpu.VMEM((2, 16, 2 * HD), BF16),
            pltpu.VMEM((16, d), F32),
            pltpu.VMEM((heads // 2, N, N * 16, rows), F32),
            pltpu.VMEM((heads // 2, N, N * 16, rows), F32),
            pltpu.VMEM((heads // 2, N, rows), F32),
            pltpu.VMEM((heads // 2, N, rows), F32),
            pltpu.VMEM((heads // 2, N, rows), F32),
            pltpu.VMEM((heads // 2, 1, rows), F32),
            pltpu.VMEM((3, 16, d // 4), BF16),
            pltpu.SMEM((1,), jnp.int32),
            pltpu.SemaphoreType.DMA((3,)),
            pltpu.SemaphoreType.DMA((4,)),
            pltpu.SemaphoreType.DMA((2, 2)),
            pltpu.SemaphoreType.DMA((4, 2, N)),
            pltpu.SemaphoreType.DMA((4, 2, N)),
            pltpu.SemaphoreType.DMA((3,)),
            pltpu.SemaphoreType.DMA((3,)),
        ],
        compiler_params=pltpu.CompilerParams(
            collective_id=0, has_side_effects=True, vmem_limit_bytes=60 * 1024 * 1024
        ),
    )(queries, d_out, prefix_keys, prefix_values, k_weight, v_weight, lengths)
    return pl.pallas_call(
        finish,
        name="sum_of_heads",
        out_shape=(shard, shard, jax.ShapeDtypeStruct((16, d // 4), BF16)),
        in_specs=[vmem] * 4,
        out_specs=(vmem,) * 3,
    )(*parts)


def solution(mesh):
    placed = (
        P("resp", "head"),
        P("resp", "head"),
        P("resp", "head"),
        P("resp", "head"),
        P(None, "head"),
        P(None, "head"),
        P("resp"),
    )
    return jax.shard_map(
        body,
        mesh=mesh,
        in_specs=placed,
        out_specs=(P("resp", "head"), P("resp", "head"), P("resp", "head")),
        check_vma=False,
    )
```

```python
import functools
import math

import jax
import jax.numpy as jnp
from jax import lax
from jax.experimental import pallas as pl
from jax.experimental.pallas import tpu as pltpu
from jax.sharding import PartitionSpec as P

HD = 128
NY, NX, NZ = 2, 4, 8
NC = 2
CHUNK = 128
N = 8
MESH = pl.DeviceIdType.MESH
SCALE = HD ** (-0.5)
LOG2E = math.log2(math.e)
F32 = jnp.float32
BF16 = jnp.bfloat16


def place():
    r = lax.axis_index("resp")
    return r // (NX * NZ), (r // NZ) % NX, r % NZ, lax.axis_index("head")


def xy_peer(i):
    y, x, z, h = place()
    return ((y + i // NX) % NY * (NX * NZ) + (x + i % NX) % NX * NZ + z, h)


def xy_back(i):
    return i // NX * NX + (-i) % NX


def z_peer(i):
    y, x, z, h = place()
    return (y * (NX * NZ) + x * NZ + (z + i) % NZ, h)


def z_back(i):
    return (-i) % NZ


XY = (xy_peer, xy_back)
Z = (z_peer, z_back)


FAR_FIRST = ((6, 5, 7, 2, 4, 1, 3), (4, 3, 5, 2, 6, 1, 7))


def head_peer(i):
    y, x, z, h = place()
    return (lax.axis_index("resp"), (h // NC + i // NC) % 2 * NC + (h + i) % NC)


def nt(a, b):
    return lax.dot_general(a, b, (((1,), (1,)), ((), ())), preferred_element_type=F32)


def send(src, dst, ss, rs, to):
    copy = pltpu.make_async_remote_copy(
        src_ref=src, dst_ref=dst, send_sem=ss, recv_sem=rs, device_id=to, device_id_type=MESH
    )
    copy.start()
    return copy


def kernel(
    q_hbm, g_hbm, k_hbm, v_hbm, kw_hbm, vw_hbm, len_hbm,
    dk_ref, dv_ref, mine_ref, theirs_ref,
    qs, gs, wts, full, outbox, inbox, partial, inbox2, low, acc,
    e_s, dp_s, m_s, l_s, w_s, d_s, hsend, len_ref,
    load_sem, own_sem, w_sem, ss, rs, hss, hrs,
):
    rows, columns = qs.shape
    group = columns // HD // 2

    barrier = pltpu.get_barrier_semaphore()
    for i in (4, 3, 5, 2, 6, 1, 7):
        pl.semaphore_signal(barrier, inc=1, device_id=z_peer(i), device_id_type=MESH)
    for i in (6, 5, 7, 2, 4, 1, 3):
        pl.semaphore_signal(barrier, inc=1, device_id=xy_peer(i), device_id_type=MESH)
    for i in range(1, 4):
        pl.semaphore_signal(barrier, inc=1, device_id=head_peer(i), device_id_type=MESH)

    own = []
    for j in range(2):
        cols = pl.ds(j * HD, HD)
        own.append(pltpu.make_async_copy(k_hbm.at[:, cols], full.at[j, 0, 0, :, pl.ds(0, HD)], own_sem.at[2 * j]))
        own.append(pltpu.make_async_copy(v_hbm.at[:, cols], full.at[j, 0, 0, :, pl.ds(HD, HD)], own_sem.at[2 * j + 1]))
    for copy in own:
        copy.start()
    loads = [
        pltpu.make_async_copy(q_hbm, qs, load_sem.at[0]),
        pltpu.make_async_copy(g_hbm, gs, load_sem.at[1]),
        pltpu.make_async_copy(len_hbm, len_ref, load_sem.at[2]),
    ]
    for copy in loads:
        copy.start()
    weights = []
    for j in (1, 0):
        for i, ref in enumerate((kw_hbm, vw_hbm)):
            weights.append(
                pltpu.make_async_copy(ref.at[:, pl.ds(j * HD, HD)], wts.at[j, :, pl.ds(i * HD, HD)], w_sem.at[j, i])
            )
    for copy in weights:
        copy.start()
    for copy in own:
        copy.wait()
    pl.semaphore_wait(barrier, 2 * (N - 1) + 3)

    sent = []

    def fan(step, j, axes, src_of, dst_of):
        peer, back = axes
        copies = []
        for i in FAR_FIRST[axes is Z]:
            copies.append(
                send(src_of(i), dst_of(back(i)), ss.at[step, j, i], rs.at[step, j, back(i)], peer(i))
            )
        sent.extend(copies)
        return copies

    spread_b = fan(0, 1, Z, lambda i: full.at[1, 0, 0], lambda b: full.at[1, 0, b])
    spread_a = fan(0, 0, XY, lambda i: full.at[0, 0, 0], lambda b: full.at[0, b, 0])
    for copy in spread_b:
        copy.wait_recv()
    fan(1, 1, XY, lambda i: full.at[1, 0], lambda b: full.at[1, b])
    for copy in spread_a:
        copy.wait_recv()
    blocks_a = fan(1, 0, Z, lambda i: full.at[0, :, 0], lambda b: full.at[0, :, b])

    for copy in loads:
        copy.wait()
    length = len_ref[0]
    slab = 16

    def mask(i, carry):
        base = pl.multiple_of(i * slab, slab)
        live = lax.broadcasted_iota(jnp.int32, (slab, columns), 0) + base < length
        grad = gs[pl.ds(base, slab), :]
        gs[pl.ds(base, slab), :] = jnp.where(live, grad.astype(F32), 0.0).astype(BF16)
        return carry

    lax.fori_loop(0, rows // slab, mask, 0)

    def head(ref, j, h):
        return ref[:, (j * group + h) * HD:(j * group + h + 1) * HD]

    def stacked(ref, j):
        return jnp.concatenate([head(ref, j, h) for h in range(group)], axis=0)

    def softmax_terms(j, first, count):
        kv = full[j, pl.ds(first, count)].reshape(count * CHUNK, 2 * HD)
        for h in range(group):
            scores = nt(kv[:, :HD], head(qs, j, h)) * (SCALE * LOG2E)
            dprobs = nt(kv[:, HD:], head(gs, j, h))
            for i in range(count):
                c = first + i
                s = scores[i * CHUNK:(i + 1) * CHUNK]
                dp = dprobs[i * CHUNK:(i + 1) * CHUNK]
                m = jnp.max(s, axis=0, keepdims=True)
                e = jnp.exp2(s - m)
                m_s[h, pl.ds(c, 1)] = m
                l_s[h, pl.ds(c, 1)] = jnp.sum(e, axis=0, keepdims=True)
                w_s[h, pl.ds(c, 1)] = jnp.sum(e * dp, axis=0, keepdims=True)
                e_s[h, c] = e
                dp_s[h, c] = dp

    def combine():
        m = m_s[...]
        f = jnp.exp2(m - jnp.max(m, axis=1, keepdims=True))
        total = jnp.sum(f * l_s[...], axis=1, keepdims=True)
        d_s[...] = jnp.sum(f * w_s[...], axis=1, keepdims=True) / total
        m_s[...] = f / total

    def block(j, c):
        back = c // NX * NX + (NX - c % NX) % NX
        return pltpu.make_async_remote_copy(
            src_ref=outbox.at[j, c], dst_ref=inbox.at[j, back],
            send_sem=ss.at[2, j, c], recv_sem=rs.at[2, j, back],
            device_id=xy_peer(c), device_id_type=MESH,
        )

    def gradients(j, count):
        def one(step, carry):
            first = N - count * (step + 1)
            probs = []
            dscores = []
            for h in range(group):
                for i in range(count):
                    p = e_s[h, first + i] * m_s[h, pl.ds(first + i, 1)]
                    probs.append(p.astype(BF16))
                    dscores.append((p * (dp_s[h, first + i] - d_s[h])).astype(BF16))

            def whole(parts):
                columns = [jnp.concatenate(parts[h * count:(h + 1) * count], axis=0) for h in range(group)]
                return jnp.concatenate(columns, axis=1)

            dv = jnp.dot(whole(probs), stacked(gs, j), preferred_element_type=F32)
            dk = jnp.dot(whole(dscores), stacked(qs, j), preferred_element_type=F32)
            span = pl.ds(first, count)
            outbox[j, span, :, :, :HD] = (dk * SCALE).astype(BF16).reshape(count, N, 16, HD)
            outbox[j, span, :, :, HD:] = dv.astype(BF16).reshape(count, N, 16, HD)
            for i in range(count - 1, 0, -1):
                block(j, first + i).start()

            @pl.when(first > 0)
            def _():
                block(j, first).start()

            return carry

        lax.fori_loop(0, N // count, one, 0)

    def reduce1(j):
        total = outbox[j, 0].astype(F32)
        for i in range(N - 1, 0, -1):
            block(j, i).wait_recv()
            total += inbox[j, xy_back(i)].astype(F32)
        partial[j] = total.astype(BF16)
        return fan(3, j, Z, lambda i: partial.at[j, i], lambda b: inbox2.at[j, b])

    def reduce2(j, copies):
        total = partial[j, 0].astype(F32)
        for i, copy in zip(FAR_FIRST[1], copies):
            copy.wait_recv()
            total += inbox2[j, z_back(i)].astype(F32)
        total = total.astype(BF16)
        cols = slice(j * HD, (j + 1) * HD)
        low[j] = total
        dk_ref[:, cols] = total[:, :HD]
        dv_ref[:, cols] = total[:, HD:]

    def stream(c, carry):
        @pl.when(c > 0)
        def _():
            pltpu.make_async_remote_copy(
                src_ref=full.at[1, 0], dst_ref=full.at[1, c],
                send_sem=ss.at[1, 1, c], recv_sem=rs.at[1, 1, c],
                device_id=xy_peer(c), device_id_type=MESH,
            ).wait_recv()

        softmax_terms(1, c, 1)
        return carry

    lax.fori_loop(0, N, stream, 0)
    combine()
    gradients(1, 2)
    for copy in blocks_a:
        copy.wait_recv()

    def rest(i, carry):
        softmax_terms(0, i * 4, 4)
        return carry

    lax.fori_loop(0, N // 4, rest, 0)
    combine()
    gradients(0, 2)
    sums_b = reduce1(1)
    sums_a = reduce1(0)
    reduce2(1, sums_b)
    for copy in weights:
        copy.wait()

    def flush():
        for copy in sent[:-2 * (N - 1)]:
            copy.wait_send()

        def flushed(c, carry):
            block(1, c).wait_send()
            block(0, c).wait_send()
            return carry

        lax.fori_loop(1, N, flushed, 0)

    width = acc.shape[1] // 4
    step = 512
    low_b = low[1]

    def project(t, carry):
        span = pl.ds(pl.multiple_of(t * step, step), step)
        acc[:, span] = nt(low_b, wts[1, span, :])
        return carry

    lax.fori_loop(0, 4 * width // step, project, 0)
    flush()
    reduce2(0, sums_a)
    low_a = low[0]
    exchange = []
    for i in (2, 3, 1, 0):
        _, dest = head_peer(i)
        for t in range(width // step):
            span = pl.ds(pl.multiple_of(dest * width + t * step, step), step)
            part = acc[:, span] + nt(low_a, wts[0, span, :])
            if i:
                hsend[i - 1, :, t * step:(t + 1) * step] = part.astype(BF16)
            else:
                mine_ref[:, t * step:(t + 1) * step] = part
        if i:
            exchange.append(
                send(hsend.at[i - 1], theirs_ref.at[i - 1], hss.at[i - 1], hrs.at[i - 1], head_peer(i))
            )
    for copy in exchange:
        copy.wait_recv()
    for copy in sent[-2 * (N - 1):] + exchange:
        copy.wait_send()


def finish(dk_ref, dv_ref, mine_ref, theirs_ref, dk_out, dv_out, in_out):
    dk_out[...] = dk_ref[...]
    dv_out[...] = dv_ref[...]
    total = mine_ref[...]
    for i in range(3):
        total += theirs_ref[i].astype(F32)
    in_out[...] = total.astype(BF16)


def body(queries, d_out, prefix_keys, prefix_values, k_weight, v_weight, lengths):
    rows, width = queries.shape
    heads = width // HD
    d = k_weight.shape[0]
    hbm = pl.BlockSpec(memory_space=pltpu.HBM)
    vmem = pl.BlockSpec(memory_space=pltpu.VMEM)
    shard = jax.ShapeDtypeStruct(prefix_keys.shape, BF16)
    parts = pl.pallas_call(
        kernel,
        name="prefix_gradients",
        out_shape=(
            shard,
            shard,
            jax.ShapeDtypeStruct((16, d // 4), F32),
            jax.ShapeDtypeStruct((3, 16, d // 4), BF16),
        ),
        in_specs=[hbm] * 7,
        out_specs=(vmem,) * 4,
        scratch_shapes=[
            pltpu.VMEM((rows, width), BF16),
            pltpu.VMEM((rows, width), BF16),
            pltpu.VMEM((2, d, 2 * HD), BF16),
            pltpu.VMEM((2, N, N, 16, 2 * HD), BF16),
            pltpu.VMEM((2, N, N, 16, 2 * HD), BF16),
            pltpu.VMEM((2, N, N, 16, 2 * HD), BF16),
            pltpu.VMEM((2, N, 16, 2 * HD), BF16),
            pltpu.VMEM((2, N, 16, 2 * HD), BF16),
            pltpu.VMEM((2, 16, 2 * HD), BF16),
            pltpu.VMEM((16, d), F32),
            pltpu.VMEM((heads // 2, N, N * 16, rows), F32),
            pltpu.VMEM((heads // 2, N, N * 16, rows), F32),
            pltpu.VMEM((heads // 2, N, rows), F32),
            pltpu.VMEM((heads // 2, N, rows), F32),
            pltpu.VMEM((heads // 2, N, rows), F32),
            pltpu.VMEM((heads // 2, 1, rows), F32),
            pltpu.VMEM((3, 16, d // 4), BF16),
            pltpu.SMEM((1,), jnp.int32),
            pltpu.SemaphoreType.DMA((3,)),
            pltpu.SemaphoreType.DMA((4,)),
            pltpu.SemaphoreType.DMA((2, 2)),
            pltpu.SemaphoreType.DMA((4, 2, N)),
            pltpu.SemaphoreType.DMA((4, 2, N)),
            pltpu.SemaphoreType.DMA((3,)),
            pltpu.SemaphoreType.DMA((3,)),
        ],
        compiler_params=pltpu.CompilerParams(
            collective_id=0, has_side_effects=True, vmem_limit_bytes=60 * 1024 * 1024
        ),
    )(queries, d_out, prefix_keys, prefix_values, k_weight, v_weight, lengths)
    return pl.pallas_call(
        finish,
        name="sum_of_heads",
        out_shape=(shard, shard, jax.ShapeDtypeStruct((16, d // 4), BF16)),
        in_specs=[vmem] * 4,
        out_specs=(vmem,) * 3,
    )(*parts)


def solution(mesh):
    placed = (
        P("resp", "head"),
        P("resp", "head"),
        P("resp", "head"),
        P("resp", "head"),
        P(None, "head"),
        P(None, "head"),
        P("resp"),
    )
    return jax.shard_map(
        body,
        mesh=mesh,
        in_specs=placed,
        out_specs=(P("resp", "head"), P("resp", "head"), P("resp", "head")),
        check_vma=False,
    )
```

```python
import functools
import math

import jax
import jax.numpy as jnp
from jax import lax
from jax.experimental import pallas as pl
from jax.experimental.pallas import tpu as pltpu
from jax.sharding import PartitionSpec as P

HD = 128
NY, NX, NZ = 2, 4, 8
NC = 2
CHUNK = 128
N = 8
MESH = pl.DeviceIdType.MESH
SCALE = HD ** (-0.5)
LOG2E = math.log2(math.e)
F32 = jnp.float32
BF16 = jnp.bfloat16


def place():
    r = lax.axis_index("resp")
    return r // (NX * NZ), (r // NZ) % NX, r % NZ, lax.axis_index("head")


def xy_peer(i):
    y, x, z, h = place()
    return ((y + i // NX) % NY * (NX * NZ) + (x + i % NX) % NX * NZ + z, h)


def xy_back(i):
    return i // NX * NX + (-i) % NX


def z_peer(i):
    y, x, z, h = place()
    return (y * (NX * NZ) + x * NZ + (z + i) % NZ, h)


def z_back(i):
    return (-i) % NZ


XY = (xy_peer, xy_back)
Z = (z_peer, z_back)


def head_peer(i):
    y, x, z, h = place()
    return (lax.axis_index("resp"), (h // NC + i // NC) % 2 * NC + (h + i) % NC)


def nt(a, b):
    return lax.dot_general(a, b, (((1,), (1,)), ((), ())), preferred_element_type=F32)


def send(src, dst, ss, rs, to):
    copy = pltpu.make_async_remote_copy(
        src_ref=src, dst_ref=dst, send_sem=ss, recv_sem=rs, device_id=to, device_id_type=MESH
    )
    copy.start()
    return copy


def kernel(
    q_hbm, g_hbm, k_hbm, v_hbm, kw_hbm, vw_hbm, len_hbm,
    dk_ref, dv_ref, mine_ref, theirs_ref,
    qs, gs, wts, full, outbox, inbox, partial, inbox2, low, acc,
    e_s, dp_s, m_s, l_s, w_s, d_s, hsend, len_ref,
    load_sem, own_sem, w_sem, ss, rs, hss, hrs,
):
    rows, columns = qs.shape
    group = columns // HD // 2

    barrier = pltpu.get_barrier_semaphore()
    for peer, _ in (XY, Z):
        for i in range(1, N):
            pl.semaphore_signal(barrier, inc=1, device_id=peer(i), device_id_type=MESH)
    for i in range(1, 4):
        pl.semaphore_signal(barrier, inc=1, device_id=head_peer(i), device_id_type=MESH)

    own = []
    for j in range(2):
        cols = pl.ds(j * HD, HD)
        own.append(pltpu.make_async_copy(k_hbm.at[:, cols], full.at[j, 0, 0, :, pl.ds(0, HD)], own_sem.at[2 * j]))
        own.append(pltpu.make_async_copy(v_hbm.at[:, cols], full.at[j, 0, 0, :, pl.ds(HD, HD)], own_sem.at[2 * j + 1]))
    for copy in own:
        copy.start()
    loads = [
        pltpu.make_async_copy(q_hbm, qs, load_sem.at[0]),
        pltpu.make_async_copy(g_hbm, gs, load_sem.at[1]),
        pltpu.make_async_copy(len_hbm, len_ref, load_sem.at[2]),
    ]
    for copy in loads:
        copy.start()
    weights = []
    for j in (1, 0):
        for i, ref in enumerate((kw_hbm, vw_hbm)):
            weights.append(
                pltpu.make_async_copy(ref.at[:, pl.ds(j * HD, HD)], wts.at[j, :, pl.ds(i * HD, HD)], w_sem.at[j, i])
            )
    for copy in weights:
        copy.start()
    for copy in own:
        copy.wait()
    pl.semaphore_wait(barrier, 2 * (N - 1) + 3)

    sent = []

    def fan(step, j, axes, src_of, dst_of):
        peer, back = axes
        copies = []
        for i in range(1, N):
            copies.append(
                send(src_of(i), dst_of(back(i)), ss.at[step, j, i], rs.at[step, j, back(i)], peer(i))
            )
        sent.extend(copies)
        return copies

    spread_b = fan(0, 1, Z, lambda i: full.at[1, 0, 0], lambda b: full.at[1, 0, b])
    spread_a = fan(0, 0, XY, lambda i: full.at[0, 0, 0], lambda b: full.at[0, b, 0])
    for copy in loads:
        copy.wait()
    length = len_ref[0]
    slab = 16

    def mask(i, carry):
        base = pl.multiple_of(i * slab, slab)
        live = lax.broadcasted_iota(jnp.int32, (slab, columns), 0) + base < length
        grad = gs[pl.ds(base, slab), :]
        gs[pl.ds(base, slab), :] = jnp.where(live, grad.astype(F32), 0.0).astype(BF16)
        return carry

    lax.fori_loop(0, rows // slab, mask, 0)

    for copy in spread_b:
        copy.wait_recv()
    fan(1, 1, XY, lambda i: full.at[1, 0], lambda b: full.at[1, b])
    for copy in spread_a:
        copy.wait_recv()
    blocks_a = fan(1, 0, Z, lambda i: full.at[0, :, 0], lambda b: full.at[0, :, b])

    def head(ref, j, h):
        return ref[:, (j * group + h) * HD:(j * group + h + 1) * HD]

    def stacked(ref, j):
        return jnp.concatenate([head(ref, j, h) for h in range(group)], axis=0)

    def softmax_terms(j, first, count):
        kv = full[j, pl.ds(first, count)].reshape(count * CHUNK, 2 * HD)
        for h in range(group):
            scores = nt(kv[:, :HD], head(qs, j, h)) * (SCALE * LOG2E)
            dprobs = nt(kv[:, HD:], head(gs, j, h))
            for i in range(count):
                c = first + i
                s = scores[i * CHUNK:(i + 1) * CHUNK]
                dp = dprobs[i * CHUNK:(i + 1) * CHUNK]
                m = jnp.max(s, axis=0, keepdims=True)
                e = jnp.exp2(s - m)
                m_s[h, pl.ds(c, 1)] = m
                l_s[h, pl.ds(c, 1)] = jnp.sum(e, axis=0, keepdims=True)
                w_s[h, pl.ds(c, 1)] = jnp.sum(e * dp, axis=0, keepdims=True)
                e_s[h, c] = e
                dp_s[h, c] = dp

    def combine():
        m = m_s[...]
        f = jnp.exp2(m - jnp.max(m, axis=1, keepdims=True))
        total = jnp.sum(f * l_s[...], axis=1, keepdims=True)
        d_s[...] = jnp.sum(f * w_s[...], axis=1, keepdims=True) / total
        m_s[...] = f / total

    def block(j, c):
        back = c // NX * NX + (NX - c % NX) % NX
        return pltpu.make_async_remote_copy(
            src_ref=outbox.at[j, c], dst_ref=inbox.at[j, back],
            send_sem=ss.at[2, j, c], recv_sem=rs.at[2, j, back],
            device_id=xy_peer(c), device_id_type=MESH,
        )

    def gradients(j, count):
        def one(step, carry):
            first = N - count * (step + 1)
            probs = []
            dscores = []
            for h in range(group):
                for i in range(count):
                    p = e_s[h, first + i] * m_s[h, pl.ds(first + i, 1)]
                    probs.append(p.astype(BF16))
                    dscores.append((p * (dp_s[h, first + i] - d_s[h])).astype(BF16))

            def whole(parts):
                columns = [jnp.concatenate(parts[h * count:(h + 1) * count], axis=0) for h in range(group)]
                return jnp.concatenate(columns, axis=1)

            dv = jnp.dot(whole(probs), stacked(gs, j), preferred_element_type=F32)
            dk = jnp.dot(whole(dscores), stacked(qs, j), preferred_element_type=F32)
            span = pl.ds(first, count)
            outbox[j, span, :, :, :HD] = (dk * SCALE).astype(BF16).reshape(count, N, 16, HD)
            outbox[j, span, :, :, HD:] = dv.astype(BF16).reshape(count, N, 16, HD)
            for i in range(count - 1, 0, -1):
                block(j, first + i).start()

            @pl.when(first > 0)
            def _():
                block(j, first).start()

            return carry

        lax.fori_loop(0, N // count, one, 0)

    def reduce1(j):
        total = outbox[j, 0].astype(F32)
        for i in range(N - 1, 0, -1):
            block(j, i).wait_recv()
            total += inbox[j, xy_back(i)].astype(F32)
        partial[j] = total.astype(BF16)
        return fan(3, j, Z, lambda i: partial.at[j, i], lambda b: inbox2.at[j, b])

    def reduce2(j, copies):
        total = partial[j, 0].astype(F32)
        for i, copy in enumerate(copies):
            copy.wait_recv()
            total += inbox2[j, z_back(i + 1)].astype(F32)
        total = total.astype(BF16)
        cols = slice(j * HD, (j + 1) * HD)
        low[j] = total
        dk_ref[:, cols] = total[:, :HD]
        dv_ref[:, cols] = total[:, HD:]

    def stream(c, carry):
        @pl.when(c > 0)
        def _():
            pltpu.make_async_remote_copy(
                src_ref=full.at[1, 0], dst_ref=full.at[1, c],
                send_sem=ss.at[1, 1, c], recv_sem=rs.at[1, 1, c],
                device_id=xy_peer(c), device_id_type=MESH,
            ).wait_recv()

        softmax_terms(1, c, 1)
        return carry

    lax.fori_loop(0, N, stream, 0)
    combine()
    gradients(1, 4)
    for copy in blocks_a:
        copy.wait_recv()

    def rest(i, carry):
        softmax_terms(0, i * 4, 4)
        return carry

    lax.fori_loop(0, N // 4, rest, 0)
    combine()
    gradients(0, 4)
    sums_b = reduce1(1)
    sums_a = reduce1(0)
    reduce2(1, sums_b)
    for copy in weights:
        copy.wait()

    def flush():
        for copy in sent[:-2 * (N - 1)]:
            copy.wait_send()

        def flushed(c, carry):
            block(1, c).wait_send()
            block(0, c).wait_send()
            return carry

        lax.fori_loop(1, N, flushed, 0)

    width = acc.shape[1] // 4
    step = 512
    low_b = low[1]

    def project(t, carry):
        span = pl.ds(pl.multiple_of(t * step, step), step)
        acc[:, span] = nt(low_b, wts[1, span, :])
        return carry

    lax.fori_loop(0, 4 * width // step, project, 0)
    flush()
    reduce2(0, sums_a)
    low_a = low[0]
    exchange = []
    for i in (2, 3, 1, 0):
        _, dest = head_peer(i)
        for t in range(width // step):
            span = pl.ds(pl.multiple_of(dest * width + t * step, step), step)
            part = acc[:, span] + nt(low_a, wts[0, span, :])
            if i:
                hsend[i - 1, :, t * step:(t + 1) * step] = part.astype(BF16)
            else:
                mine_ref[:, t * step:(t + 1) * step] = part
        if i:
            exchange.append(
                send(hsend.at[i - 1], theirs_ref.at[i - 1], hss.at[i - 1], hrs.at[i - 1], head_peer(i))
            )
    for copy in exchange:
        copy.wait_recv()
    for copy in sent[-2 * (N - 1):] + exchange:
        copy.wait_send()


def finish(dk_ref, dv_ref, mine_ref, theirs_ref, dk_out, dv_out, in_out):
    dk_out[...] = dk_ref[...]
    dv_out[...] = dv_ref[...]
    total = mine_ref[...]
    for i in range(3):
        total += theirs_ref[i].astype(F32)
    in_out[...] = total.astype(BF16)


def body(queries, d_out, prefix_keys, prefix_values, k_weight, v_weight, lengths):
    rows, width = queries.shape
    heads = width // HD
    d = k_weight.shape[0]
    hbm = pl.BlockSpec(memory_space=pltpu.HBM)
    vmem = pl.BlockSpec(memory_space=pltpu.VMEM)
    shard = jax.ShapeDtypeStruct(prefix_keys.shape, BF16)
    parts = pl.pallas_call(
        kernel,
        name="prefix_gradients",
        out_shape=(
            shard,
            shard,
            jax.ShapeDtypeStruct((16, d // 4), F32),
            jax.ShapeDtypeStruct((3, 16, d // 4), BF16),
        ),
        in_specs=[hbm] * 7,
        out_specs=(vmem,) * 4,
        scratch_shapes=[
            pltpu.VMEM((rows, width), BF16),
            pltpu.VMEM((rows, width), BF16),
            pltpu.VMEM((2, d, 2 * HD), BF16),
            pltpu.VMEM((2, N, N, 16, 2 * HD), BF16),
            pltpu.VMEM((2, N, N, 16, 2 * HD), BF16),
            pltpu.VMEM((2, N, N, 16, 2 * HD), BF16),
            pltpu.VMEM((2, N, 16, 2 * HD), BF16),
            pltpu.VMEM((2, N, 16, 2 * HD), BF16),
            pltpu.VMEM((2, 16, 2 * HD), BF16),
            pltpu.VMEM((16, d), F32),
            pltpu.VMEM((heads // 2, N, N * 16, rows), F32),
            pltpu.VMEM((heads // 2, N, N * 16, rows), F32),
            pltpu.VMEM((heads // 2, N, rows), F32),
            pltpu.VMEM((heads // 2, N, rows), F32),
            pltpu.VMEM((heads // 2, N, rows), F32),
            pltpu.VMEM((heads // 2, 1, rows), F32),
            pltpu.VMEM((3, 16, d // 4), BF16),
            pltpu.SMEM((1,), jnp.int32),
            pltpu.SemaphoreType.DMA((3,)),
            pltpu.SemaphoreType.DMA((4,)),
            pltpu.SemaphoreType.DMA((2, 2)),
            pltpu.SemaphoreType.DMA((4, 2, N)),
            pltpu.SemaphoreType.DMA((4, 2, N)),
            pltpu.SemaphoreType.DMA((3,)),
            pltpu.SemaphoreType.DMA((3,)),
        ],
        compiler_params=pltpu.CompilerParams(
            collective_id=0, has_side_effects=True, vmem_limit_bytes=60 * 1024 * 1024
        ),
    )(queries, d_out, prefix_keys, prefix_values, k_weight, v_weight, lengths)
    return pl.pallas_call(
        finish,
        name="sum_of_heads",
        out_shape=(shard, shard, jax.ShapeDtypeStruct((16, d // 4), BF16)),
        in_specs=[vmem] * 4,
        out_specs=(vmem,) * 3,
    )(*parts)


def solution(mesh):
    placed = (
        P("resp", "head"),
        P("resp", "head"),
        P("resp", "head"),
        P("resp", "head"),
        P(None, "head"),
        P(None, "head"),
        P("resp"),
    )
    return jax.shard_map(
        body,
        mesh=mesh,
        in_specs=placed,
        out_specs=(P("resp", "head"), P("resp", "head"), P("resp", "head")),
        check_vma=False,
    )
```
